32 devices in a mesh: band: 8 (over z, x), rows: 4 (over y, core).
Axes of the slice: x: 2, y: 2, z: 4, core: 2. Of those that a mesh axis runs over, the one named last changes fastest.
Arguments:
- latents: bfloat16 [33280, 16], P(('band', 'rows')), may hold values from -6 to 6
- token_cell: int32 [33280], P(('band', 'rows')), may hold values from 0 to 33279, as said below
- frame_counts: int32 [8], replicated, may hold values from 1 to 4, 13 in all
- in_kernel: bfloat16 [3, 3, 3, 16, 384], replicated, may hold values from -0.3125 to 0.3125
- in_bias: float32 [384], replicated, may hold values from -3 to 3
- mid_kernel: bfloat16 [3, 3, 3, 384, 384], replicated, may hold values from -0.0625 to 0.0625
- mid_bias: float32 [384], replicated, may hold values from -3 to 3
Outputs:
- decoded: bfloat16 [32, 16, 160, 384], P('band', 'rows')
The draws below stay inside these ranges and needn't reach their ends.
Inputs may be any that keep to these rules, and one draw needn't show every extreme that they name: `token_cell`: rows d * 1040 to (d + 1) * 1040 - 1 (d the flat index over band+rows) are, in some order, the cells f * 16 * 160 + d * 80 + s for every f < 13 and s < 80, each once. `frame_counts`: the counts sum to 13; some band holds 4 frames.
All inputs are finite; a program needn't handle non-finite values.
Results may differ from the reference program's by a relative error of at most 0.0043.
Values may be sent and summed in bfloat16 or wider, within the bound.
A program may use at most 64 MiB of HBM per device.

```python
import math
import jax
import jax.numpy as jnp
import numpy as np
from jax import lax

Z = 16
C = 384
W = 160
FCAP = 4
FRAMES = 13
H = 16
SPAN = 80
TOK_DEV = 1040
TOKENS = 33280
N_BAND = 8


def draw_token_cell(key, part):
    devices = TOKENS // TOK_DEV
    subkeys = jax.random.split(key, devices)

    def shuffle(subkey):
        return jax.random.permutation(subkey, TOK_DEV)
    local_order = jax.vmap(shuffle)(subkeys).astype(jnp.int32)
    device_ids = jnp.arange(devices, dtype=jnp.int32)[:, None]
    cells = local_order // SPAN * (H * W) + device_ids * SPAN + local_order % SPAN
    return cells.reshape(-1).astype(jnp.int32)


def levels(key, shape, cuts, smallest, high):
    level, own = 1.0, jax.random.fold_in(key, 6)
    for dim, shards_of in cuts:
        steps = jnp.exp(jax.random.uniform(jax.random.fold_in(own, dim), (shards_of,), jnp.float32, smallest / len(cuts), high / len(cuts)))
        level = level * jnp.repeat(steps, shape[dim] // shards_of).reshape([-1 if axis == dim else 1 for axis in range(len(shape))])
    return level


def split_up(number_of, total, bound, lean):
    weights = [(1 << 20) // math.isqrt(rank ** lean) + 1 for rank in range(2, number_of + 1)]
    surplus, holding = total - bound - (number_of - 1), [1] * (number_of - 1)
    while surplus > 0:
        candidates = [i for i in range(number_of - 1) if holding[i] < bound]
        mass, remaining = sum([weights[i] for i in candidates]), surplus
        for i in candidates:
            extra = min(bound - holding[i], max(1, remaining * weights[i] // mass), surplus)
            holding[i] = holding[i] + extra
            surplus = surplus - extra
    return np.array([bound] + holding)


def ragged(stream_key, amount, total, bound, skew):
    if amount == 2:
        one = jax.random.randint(stream_key, (), max(1, total - bound), min(bound, total - 1) + 1)
        return jnp.stack([one, total - one])
    sizes = jnp.asarray(split_up(amount, total, bound, skew), jnp.int32)
    couples = (amount - 1) // 2
    source_of, sink = sizes[1:1 + 2 * couples:2], sizes[2:2 + 2 * couples:2]
    slack = jnp.minimum(source_of - 1, bound - sink)
    moved = jax.random.randint(jax.random.fold_in(stream_key, 1), (couples,), 0, 1 << 20) % (slack + 1)
    sizes = sizes.at[1:1 + 2 * couples:2].set(source_of - moved).at[2:2 + 2 * couples:2].set(sink + moved)
    return sizes[jax.random.permutation(jax.random.fold_in(stream_key, 2), amount)]


def noise(rng, shape, deviation, limit, cuts=(), kind=jnp.bfloat16):
    gain = levels(rng, shape, cuts, -0.22, 0.18) if cuts else 1.0
    values = jax.random.normal(rng, shape, jnp.float32) * deviation * gain
    return jnp.minimum(jnp.maximum(values, -limit), limit).astype(kind)


def setup_inputs(seed: int = 0) -> dict:
    streams_of = jax.random.split(jax.random.key(seed), 8)
    return {
        "latents": noise(streams_of[0], (TOKENS, Z), 1.0, 6.0, ((0, 32),)),
        "token_cell": draw_token_cell(jax.random.fold_in(streams_of[7], 71), 0),
        "frame_counts": ragged(streams_of[2], N_BAND, FRAMES, FCAP, 2).astype(jnp.int32),
        "in_kernel": noise(streams_of[3], (3, 3, 3, Z, C), (27 * Z) ** -0.5, 0.3125),
        "in_bias": noise(streams_of[4], (C,), 0.5, 3.0, (), jnp.float32),
        "mid_kernel": noise(streams_of[5], (3, 3, 3, C, C), (27 * C) ** -0.5, 0.0625),
        "mid_bias": noise(streams_of[6], (C,), 0.5, 3.0, (), jnp.float32),
    }


conv_layout = ("NDHWC", "DHWIO", "NDHWC")


def causal_conv(volume, kernel, bias):
    summed = lax.conv_general_dilated(volume[None], kernel, (1, 1, 1), [(2, 0), (1, 1), (1, 1)], dimension_numbers=conv_layout, preferred_element_type=jnp.float32)[0]
    return summed + bias


def reference(latents, token_cell, frame_counts, in_kernel, in_bias, mid_kernel, mid_bias):
    channels = latents.shape[1]
    grid = jnp.zeros((FRAMES * H * W, channels), latents.dtype).at[token_cell].set(latents)
    grid = grid.reshape(FRAMES, H, W, channels)
    first_conv = causal_conv(grid, in_kernel, in_bias)
    active = jax.nn.silu(first_conv).astype(jnp.bfloat16)
    mixed = causal_conv(active, mid_kernel, mid_bias).astype(jnp.bfloat16)
    counts = frame_counts.astype(jnp.int32)
    starts = (jnp.cumsum(counts) - counts).astype(jnp.int32)
    slots = jnp.arange(FCAP, dtype=jnp.int32)
    frame_index = (starts[:, None] + slots[None, :]).reshape(-1).astype(jnp.int32)
    live_slots = (slots[None, :] < counts[:, None]).reshape(-1)
    picked = jnp.take(mixed, jnp.clip(frame_index, 0, FRAMES - 1).astype(jnp.int32), axis=0)
    zeros_like = jnp.zeros_like(picked)
    return jnp.where(live_slots[:, None, None, None], picked, zeros_like)
```

```python
import functools

import jax
import jax.numpy as jnp
from jax import lax
from jax.experimental import pallas as pl
from jax.experimental.pallas import tpu as pltpu
from jax.sharding import PartitionSpec as P

W = 160
R = 4
FCAP = 4
BACK = 2
IN_FRAMES = FCAP + 2 * BACK
IN_ROWS = R + 4
MID_FRAMES = FCAP + BACK
MID_ROWS = R + 2
LANES = 128
MESH = pl.DeviceIdType.MESH


def exchange_kernel(bands, rows, counts, lat, cell, out, store, send, recv, send_sem, recv_sem):
    n, channels = lat.shape
    span = R * W // bands
    parts = W // span
    frames = n // span
    plane = R * rows * W
    band = lax.axis_index("band")
    row = lax.axis_index("rows")
    me = band * rows + row
    y = lax.div(me, parts)
    part = lax.rem(me, parts)
    home = lax.div(y, R)
    y_in = lax.rem(y, R)
    near = jnp.where(y_in < 2, home - 1, home + 1)
    near_ok = (near >= 0) & (near < rows)
    slot_home = (y_in + 2) * parts + part
    slot_near = jnp.where(y_in < 2, y_in + 6, y_in - 2) * parts + part

    def source(slot):
        src_y = R * row - 2 + slot // parts
        src = src_y * parts + slot % parts
        ok = (src_y >= 0) & (src_y < R * rows) & (src != me)
        src = jnp.maximum(src, 0)
        return lax.div(src, rows), lax.rem(src, rows), ok

    barrier = pltpu.get_barrier_semaphore()
    for slot in range(IN_ROWS * parts):
        src_band, src_row, ok = source(slot)

        @pl.when(ok)
        def _():
            pl.semaphore_signal(barrier, inc=1, device_id=(src_band, src_row), device_id_type=MESH)

    cells = cell[...]
    frame = jnp.zeros_like(cells)
    for f in range(1, frames):
        frame = frame + (cells >= f * plane).astype(jnp.int32)
    lane_of = cells - frame * plane - me * span + part * span + 1
    lane_of = jnp.where(lane_of >= LANES, lane_of - LANES, lane_of)
    eye = (
        lax.broadcasted_iota(jnp.int32, (channels, channels), 0)
        == lax.broadcasted_iota(jnp.int32, (channels, channels), 1)
    )
    eye = jnp.where(eye, 1.0, 0.0).astype(jnp.bfloat16)
    across = (((1,), (1,)), ((), ()))
    lat_t = lax.dot_general(eye, lat[...], across, preferred_element_type=jnp.float32)
    by_frame = jnp.concatenate(
        [jnp.where(frame == f, lat_t, 0.0).astype(jnp.bfloat16) for f in range(frames)], axis=0
    )
    spot = lax.broadcasted_iota(jnp.int32, (LANES, n), 0) == lane_of
    spot = jnp.where(spot, 1.0, 0.0).astype(jnp.bfloat16)
    placed = lax.dot_general(by_frame, spot, across, preferred_element_type=jnp.float32)
    store[:FCAP] = jnp.zeros((FCAP, channels, LANES), jnp.bfloat16)
    store[FCAP + frames:] = jnp.zeros((FCAP, channels, LANES), jnp.bfloat16)
    store[FCAP:FCAP + frames] = placed.astype(jnp.bfloat16).reshape(frames, channels, LANES)

    here = (home == row).astype(jnp.int32) + (near == row).astype(jnp.int32)
    total = bands + jnp.where(near_ok, bands, 0) - here
    pl.semaphore_wait(barrier, total)

    def copy_to(i, target, which, slot):
        to_band = lax.rem(band + i, bands)
        return pltpu.make_async_remote_copy(
            src_ref=send.at[i],
            dst_ref=recv.at[slot],
            send_sem=send_sem.at[which, i],
            recv_sem=recv_sem.at[slot],
            device_id=(to_band, target),
            device_id_type=MESH,
        )

    for i in range(bands):
        to_band = lax.rem(band + i, bands)
        start = jnp.int32(0)
        for q in range(bands - 1):
            start = start + jnp.where(q < to_band, counts[q], 0)
        for j in range(IN_FRAMES):
            send[i, j] = store[start + j]
        for which, target, slot, ok in ((0, home, slot_home, None), (1, near, slot_near, near_ok)):
            away = jnp.bool_(True) if i else target != row
            go = away if ok is None else away & ok

            @pl.when(go)
            def _():
                copy_to(i, target, which, slot).start()

            if i == 0:
                @pl.when(target == row)
                def _():
                    recv[slot] = send[0]

    for slot in range(IN_ROWS * parts):
        src_band, src_row, ok = source(slot)

        @pl.when(ok)
        def _():
            pltpu.make_async_remote_copy(
                src_ref=send.at[0],
                dst_ref=recv.at[slot],
                send_sem=send_sem.at[0, 0],
                recv_sem=recv_sem.at[slot],
                device_id=(src_band, src_row),
                device_id_type=MESH,
            ).wait_recv()

    lane = lax.broadcasted_iota(jnp.int32, (IN_FRAMES, channels, LANES), 2)
    for yy in range(IN_ROWS):
        at = R * row - 2 + yy
        inside = (at >= 0) & (at < R * rows)

        @pl.when(inside)
        def _():
            low = recv[yy * parts].astype(jnp.float32)
            for p in range(1, parts):
                piece = recv[yy * parts + p].astype(jnp.float32)
                low = jnp.where(lane >= p * span + 1, piece, low)
            high = jnp.where(lane < W + 1 - LANES, piece, 0.0)
            out[yy, :, :, :LANES] = low.astype(jnp.bfloat16)
            out[yy, :, :, LANES:] = high.astype(jnp.bfloat16)

        @pl.when(jnp.logical_not(inside))
        def _():
            out[yy] = jnp.zeros(out.shape[1:], jnp.bfloat16)

    for i in range(bands):
        for which, target, slot, ok in ((0, home, slot_home, None), (1, near, slot_near, near_ok)):
            away = jnp.bool_(True) if i else target != row
            go = away if ok is None else away & ok

            @pl.when(go)
            def _():
                copy_to(i, target, which, slot).wait_send()


def conv_kernel(bands, rows, counts, xin, w1, b1, w2, b2, out, xs, mid, wcat, acc, obuf, w_sem, o_sem):
    channels = xin.shape[2]
    wide = w1.shape[1]
    depth = 3 * wide
    band = lax.axis_index("band")
    row = lax.axis_index("rows")

    def weight_copy(a, b):
        return pltpu.make_async_copy(
            w2.at[a, b], wcat.at[b, :, pl.ds((2 - a) * wide, wide)], w_sem.at[a, b]
        )

    for b in range(3):
        for a in range(3):
            weight_copy(a, b).start()

    start = jnp.int32(0)
    for q in range(bands - 1):
        start = start + jnp.where(q < band, counts[q], 0)
    own = counts[band]

    def shift_row(yy, carry):
        whole = xin[yy].astype(jnp.float32)
        flat = whole.reshape(IN_FRAMES * channels, 2 * LANES)
        for e in range(3):
            moved = flat if e == 0 else pltpu.roll(flat, 2 * LANES - e, 1)
            moved = moved[:, :W].astype(jnp.bfloat16)
            xs[e, yy] = moved.reshape(IN_FRAMES, channels, W)
        return carry

    lax.fori_loop(0, IN_ROWS, shift_row, 0)

    place = lax.broadcasted_iota(jnp.int32, (W, wide), 0)

    def first(i, carry):
        f = lax.div(i, MID_ROWS)
        y = lax.rem(i, MID_ROWS)
        taps = [xs[e, y + b, f + a] for a in range(3) for b in range(3) for e in range(3)]
        lhs = jnp.concatenate(taps, axis=0)
        v = lax.dot_general(
            lhs, w1[...], (((0,), (0,)), ((), ())), preferred_element_type=jnp.float32
        )
        v = v + b1[...]
        at = R * row - 1 + y
        inside = (at >= 0) & (at < R * rows) & (start - BACK + f >= 0)
        half = 0.5 * v
        active = jnp.where(inside, half * jnp.tanh(half) + half, 0.0)
        before = jnp.where(place == 0, 0.0, pltpu.roll(active, 1, 0))
        after = jnp.where(place == W - 1, 0.0, pltpu.roll(active, W - 1, 0))
        mid[f, y, :, :wide] = before.astype(jnp.bfloat16)
        mid[f, y, :, wide:2 * wide] = active.astype(jnp.bfloat16)
        mid[f, y, :, 2 * wide:] = after.astype(jnp.bfloat16)
        return carry

    lax.fori_loop(0, MID_FRAMES * MID_ROWS, first, 0)

    for b in range(3):
        for a in range(3):
            weight_copy(a, b).wait()

    for pair in range(FCAP // 2):
        acc[...] = jnp.broadcast_to(b2[...], acc.shape)

        def taps_of(b, carry):
            def rows_of(g):
                return mid[2 * pair + g, pl.ds(b, R)].reshape(R * W, depth)

            acc[:, :wide] += jnp.dot(
                rows_of(0), wcat[b, :, 2 * wide:], preferred_element_type=jnp.float32
            )
            acc[...] += jnp.dot(
                rows_of(1), wcat[b, :, wide:], preferred_element_type=jnp.float32
            )
            acc[...] += jnp.dot(
                rows_of(2), wcat[b, :, :2 * wide], preferred_element_type=jnp.float32
            )
            acc[:, wide:] += jnp.dot(
                rows_of(3), wcat[b, :, :wide], preferred_element_type=jnp.float32
            )
            return carry

        lax.fori_loop(0, 3, taps_of, 0)
        for k in range(2):
            t = 2 * pair + k
            value = acc[:, k * wide:(k + 1) * wide]
            value = jnp.where(t < own, value, 0.0).astype(jnp.bfloat16)
            obuf[t] = value.reshape(R, W, wide)
            pltpu.make_async_copy(obuf.at[t], out.at[t], o_sem.at[t]).start()
    for t in range(FCAP):
        pltpu.make_async_copy(obuf.at[t], out.at[t], o_sem.at[t]).wait()


def per_device(bands, rows, latents, token_cell, frame_counts, in_kernel, in_bias, mid_kernel, mid_bias):
    n, channels = latents.shape
    wide = in_kernel.shape[-1]
    span = R * W // bands
    parts = W // span
    frames = n // span
    vmem = pl.BlockSpec(memory_space=pltpu.VMEM)
    smem = pl.BlockSpec(memory_space=pltpu.SMEM)
    anywhere = pl.BlockSpec(memory_space=pl.ANY)
    tile = (IN_FRAMES, channels, LANES)
    xin = pl.pallas_call(
        functools.partial(exchange_kernel, bands, rows),
        out_shape=jax.ShapeDtypeStruct((IN_ROWS, IN_FRAMES, channels, 2 * LANES), jnp.bfloat16),
        in_specs=[smem, vmem, vmem],
        out_specs=vmem,
        scratch_shapes=[
            pltpu.VMEM((frames + 2 * FCAP, channels, LANES), jnp.bfloat16),
            pltpu.VMEM((bands,) + tile, jnp.bfloat16),
            pltpu.VMEM((IN_ROWS * parts,) + tile, jnp.bfloat16),
            pltpu.SemaphoreType.DMA((2, bands)),
            pltpu.SemaphoreType.DMA((IN_ROWS * parts,)),
        ],
        compiler_params=pltpu.CompilerParams(
            collective_id=0, has_side_effects=True, vmem_limit_bytes=32 * 1024 * 1024
        ),
        name="exchange",
    )(frame_counts, latents, token_cell.reshape(1, n))
    flops = 2 * FCAP * R * W * 27 * wide * wide
    return pl.pallas_call(
        functools.partial(conv_kernel, bands, rows),
        out_shape=jax.ShapeDtypeStruct((FCAP, R, W, wide), jnp.bfloat16),
        in_specs=[smem, vmem, vmem, vmem, anywhere, vmem],
        out_specs=anywhere,
        scratch_shapes=[
            pltpu.VMEM((3, IN_ROWS, IN_FRAMES, channels, W), jnp.bfloat16),
            pltpu.VMEM((MID_FRAMES, MID_ROWS, W, 3 * wide), jnp.bfloat16),
            pltpu.VMEM((3, 3 * wide, 3 * wide), jnp.bfloat16),
            pltpu.VMEM((R * W, 2 * wide), jnp.float32),
            pltpu.VMEM((FCAP, R, W, wide), jnp.bfloat16),
            pltpu.SemaphoreType.DMA((3, 3)),
            pltpu.SemaphoreType.DMA((FCAP,)),
        ],
        compiler_params=pltpu.CompilerParams(vmem_limit_bytes=56 * 1024 * 1024),
        cost_estimate=pl.CostEstimate(flops=flops, bytes_accessed=12 << 20, transcendentals=0),
        name="convs",
    )(
        frame_counts,
        xin,
        in_kernel.reshape(27 * channels, wide),
        in_bias.reshape(1, wide),
        mid_kernel.reshape(3, 3, 3 * wide, wide),
        jnp.concatenate([mid_bias, mid_bias]).reshape(1, 2 * wide),
    )


def solution(mesh):
    placed = (P(("band", "rows"), None), P(("band", "rows")), P(), P(), P(), P(), P())
    return jax.shard_map(
        functools.partial(per_device, mesh.shape["band"], mesh.shape["rows"]),
        mesh=mesh,
        in_specs=placed,
        out_specs=P("band", "rows", None, None),
        check_vma=False,
    )
```

```python
import functools

import jax
import jax.numpy as jnp
from jax import lax
from jax.experimental import pallas as pl
from jax.experimental.pallas import tpu as pltpu
from jax.sharding import PartitionSpec as P

W = 160
R = 4
FCAP = 4
BACK = 2
IN_FRAMES = FCAP + 2 * BACK
IN_ROWS = R + 4
MID_FRAMES = FCAP + BACK
MID_ROWS = R + 2
LANES = 128
MESH = pl.DeviceIdType.MESH


def exchange_kernel(
    bands, rows, counts_in, lat_in, cell_in, out,
    counts, lat, cell, store, send, recv, send_sem, recv_sem, load_sem,
):
    loads = [
        pltpu.make_async_copy(a, b, load_sem.at[i])
        for i, (a, b) in enumerate(((cell_in, cell), (lat_in, lat), (counts_in, counts)))
    ]
    for load in loads:
        load.start()
    channels, n = lat.shape
    span = R * W // bands
    parts = W // span
    frames = n // span
    plane = R * rows * W
    band = lax.axis_index("band")
    row = lax.axis_index("rows")
    me = band * rows + row
    y = lax.div(me, parts)
    part = lax.rem(me, parts)
    home = lax.div(y, R)
    y_in = lax.rem(y, R)
    near = jnp.where(y_in < 2, home - 1, home + 1)
    near_ok = (near >= 0) & (near < rows)
    slot_home = (y_in + 2) * parts + part
    slot_near = jnp.where(y_in < 2, y_in + 6, y_in - 2) * parts + part

    def source(slot):
        src_y = R * row - 2 + slot // parts
        src = src_y * parts + slot % parts
        ok = (src_y >= 0) & (src_y < R * rows) & (src != me)
        src = jnp.maximum(src, 0)
        return lax.div(src, rows), lax.rem(src, rows), ok

    barrier = pltpu.get_barrier_semaphore()
    for slot in range(IN_ROWS * parts):
        src_band, src_row, ok = source(slot)

        @pl.when(ok)
        def _():
            pl.semaphore_signal(barrier, inc=1, device_id=(src_band, src_row), device_id_type=MESH)

    for load in loads:
        load.wait()
    cells = cell[...].reshape(1, n)
    frame = jnp.zeros_like(cells)
    for f in range(1, frames):
        frame = frame + (cells >= f * plane).astype(jnp.int32)
    lane_of = cells - frame * plane - me * span + part * span + 1
    lane_of = jnp.where(lane_of >= LANES, lane_of - LANES, lane_of)
    lat_t = lat[...].astype(jnp.float32)
    across = (((1,), (1,)), ((), ()))
    by_frame = jnp.concatenate(
        [jnp.where(frame == f, lat_t, 0.0).astype(jnp.bfloat16) for f in range(frames)], axis=0
    )
    spot = lax.broadcasted_iota(jnp.int32, (LANES, n), 0) == lane_of
    spot = jnp.where(spot, 1.0, 0.0).astype(jnp.bfloat16)
    placed = lax.dot_general(by_frame, spot, across, preferred_element_type=jnp.float32)
    store[:FCAP] = jnp.zeros((FCAP, channels, LANES), jnp.bfloat16)
    store[FCAP + frames:] = jnp.zeros((FCAP, channels, LANES), jnp.bfloat16)
    store[FCAP:FCAP + frames] = placed.astype(jnp.bfloat16).reshape(frames, channels, LANES)

    here = (home == row).astype(jnp.int32) + (near == row).astype(jnp.int32)
    total = bands + jnp.where(near_ok, bands, 0) - here
    pl.semaphore_wait(barrier, total)

    def copy_to(i, target, which, slot):
        to_band = lax.rem(band + i, bands)
        return pltpu.make_async_remote_copy(
            src_ref=send.at[i],
            dst_ref=recv.at[slot],
            send_sem=send_sem.at[which, i],
            recv_sem=recv_sem.at[slot],
            device_id=(to_band, target),
            device_id_type=MESH,
        )

    for i in range(bands):
        to_band = lax.rem(band + i, bands)
        start = jnp.int32(0)
        for q in range(bands - 1):
            start = start + jnp.where(q < to_band, counts[q], 0)
        for j in range(IN_FRAMES):
            send[i, j] = store[start + j]
        for which, target, slot, ok in ((0, home, slot_home, None), (1, near, slot_near, near_ok)):
            away = jnp.bool_(True) if i else target != row
            go = away if ok is None else away & ok

            @pl.when(go)
            def _():
                copy_to(i, target, which, slot).start()

            if i == 0:
                @pl.when(target == row)
                def _():
                    recv[slot] = send[0]

    for slot in range(IN_ROWS * parts):
        src_band, src_row, ok = source(slot)

        @pl.when(ok)
        def _():
            pltpu.make_async_remote_copy(
                src_ref=send.at[0],
                dst_ref=recv.at[slot],
                send_sem=send_sem.at[0, 0],
                recv_sem=recv_sem.at[slot],
                device_id=(src_band, src_row),
                device_id_type=MESH,
            ).wait_recv()

    lane = lax.broadcasted_iota(jnp.int32, (IN_FRAMES, channels, LANES), 2)
    for yy in range(IN_ROWS):
        at = R * row - 2 + yy
        inside = (at >= 0) & (at < R * rows)

        @pl.when(inside)
        def _():
            low = recv[yy * parts].astype(jnp.float32)
            for p in range(1, parts):
                piece = recv[yy * parts + p].astype(jnp.float32)
                low = jnp.where(lane >= p * span + 1, piece, low)
            high = jnp.where(lane < W + 1 - LANES, piece, 0.0)
            out[yy, :, :, :LANES] = low.astype(jnp.bfloat16)
            out[yy, :, :, LANES:] = high.astype(jnp.bfloat16)

        @pl.when(jnp.logical_not(inside))
        def _():
            out[yy] = jnp.zeros(out.shape[1:], jnp.bfloat16)

    for i in range(bands):
        for which, target, slot, ok in ((0, home, slot_home, None), (1, near, slot_near, near_ok)):
            away = jnp.bool_(True) if i else target != row
            go = away if ok is None else away & ok

            @pl.when(go)
            def _():
                copy_to(i, target, which, slot).wait_send()


def conv_kernel(
    bands, rows, counts_in, xin, w1_in, b1_in, w2, b2_in, out,
    counts, w1, b1, b2, xs, mid, wcat, acc, obuf, load_sem, w_sem, o_sem,
):
    loads = [
        pltpu.make_async_copy(a, b, load_sem.at[i])
        for i, (a, b) in enumerate(((counts_in, counts), (w1_in, w1), (b1_in, b1), (b2_in, b2)))
    ]
    for load in loads:
        load.start()
    channels = xin.shape[2]
    wide = w1.shape[1]
    depth = 3 * wide
    band = lax.axis_index("band")
    row = lax.axis_index("rows")

    def weight_copy(a, b):
        return pltpu.make_async_copy(
            w2.at[a, b], wcat.at[b, :, pl.ds((2 - a) * wide, wide)], w_sem.at[a, b]
        )

    for b in range(3):
        for a in range(3):
            weight_copy(a, b).start()

    def shift_row(yy, carry):
        whole = xin[yy].astype(jnp.float32)
        flat = whole.reshape(IN_FRAMES * channels, 2 * LANES)
        for e in range(3):
            moved = flat if e == 0 else pltpu.roll(flat, 2 * LANES - e, 1)
            moved = moved[:, :W].astype(jnp.bfloat16)
            xs[e, yy] = moved.reshape(IN_FRAMES, channels, W)
        return carry

    lax.fori_loop(0, IN_ROWS, shift_row, 0)

    for load in loads:
        load.wait()
    start = jnp.int32(0)
    for q in range(bands - 1):
        start = start + jnp.where(q < band, counts[q], 0)
    own = counts[band]

    place = lax.broadcasted_iota(jnp.int32, (8, wide), 0)
    bias1 = b1[...].reshape(1, wide)

    def first(f, carry):
        for y in range(MID_ROWS):
            taps = [xs[e, y + b, f + a] for a in range(3) for b in range(3) for e in range(3)]
            v = lax.dot_general(
                jnp.concatenate(taps, axis=0),
                w1[...],
                (((0,), (0,)), ((), ())),
                preferred_element_type=jnp.float32,
            )
            at = R * row - 1 + y
            inside = (at >= 0) & (at < R * rows) & (start - BACK + f >= 0)
            half = (v + bias1) * jnp.where(inside, 0.5, 0.0)
            active = half * jnp.tanh(half) + half
            before = pltpu.roll(active, 1, 0)
            before = jnp.concatenate([jnp.where(place == 0, 0.0, before[:8]), before[8:]], axis=0)
            after = pltpu.roll(active, W - 1, 0)
            after = jnp.concatenate([after[:-8], jnp.where(place == 7, 0.0, after[-8:])], axis=0)
            mid[f, y, :, :wide] = before.astype(jnp.bfloat16)
            mid[f, y, :, wide:2 * wide] = active.astype(jnp.bfloat16)
            mid[f, y, :, 2 * wide:] = after.astype(jnp.bfloat16)
        return carry

    lax.fori_loop(0, MID_FRAMES, first, 0)

    for b in range(3):
        for a in range(3):
            weight_copy(a, b).wait()

    for pair in range(FCAP // 2):
        bias = jnp.broadcast_to(b2[...].reshape(1, wide), (R * W, wide))
        acc[:, :wide] = bias
        acc[:, wide:] = bias

        def taps_of(b, carry):
            def rows_of(g):
                return mid[2 * pair + g, pl.ds(b, R)].reshape(R * W, depth)

            acc[:, :wide] += jnp.dot(
                rows_of(0), wcat[b, :, 2 * wide:], preferred_element_type=jnp.float32
            )
            acc[...] += jnp.dot(
                rows_of(1), wcat[b, :, wide:], preferred_element_type=jnp.float32
            )
            acc[...] += jnp.dot(
                rows_of(2), wcat[b, :, :2 * wide], preferred_element_type=jnp.float32
            )
            acc[:, wide:] += jnp.dot(
                rows_of(3), wcat[b, :, :wide], preferred_element_type=jnp.float32
            )
            return carry

        lax.fori_loop(0, 3, taps_of, 0)
        for k in range(2):
            t = 2 * pair + k
            value = acc[:, k * wide:(k + 1) * wide]
            value = jnp.where(t < own, value, 0.0).astype(jnp.bfloat16)
            obuf[t] = value.reshape(R, W, wide)
            pltpu.make_async_copy(obuf.at[t], out.at[t], o_sem.at[t]).start()
    for t in range(FCAP):
        pltpu.make_async_copy(obuf.at[t], out.at[t], o_sem.at[t]).wait()


def per_device(bands, rows, latents, token_cell, frame_counts, in_kernel, in_bias, mid_kernel, mid_bias):
    n, channels = latents.shape
    wide = in_kernel.shape[-1]
    span = R * W // bands
    parts = W // span
    frames = n // span
    vmem = pl.BlockSpec(memory_space=pltpu.VMEM)
    hbm = pl.BlockSpec(memory_space=pltpu.HBM)
    tile = (IN_FRAMES, channels, LANES)
    xin = pl.pallas_call(
        functools.partial(exchange_kernel, bands, rows),
        out_shape=jax.ShapeDtypeStruct((IN_ROWS, IN_FRAMES, channels, 2 * LANES), jnp.bfloat16),
        in_specs=[hbm] * 3,
        out_specs=vmem,
        scratch_shapes=[
            pltpu.SMEM((bands,), jnp.int32),
            pltpu.VMEM((channels, n), jnp.bfloat16),
            pltpu.VMEM((n,), jnp.int32),
            pltpu.VMEM((frames + 2 * FCAP, channels, LANES), jnp.bfloat16),
            pltpu.VMEM((bands,) + tile, jnp.bfloat16),
            pltpu.VMEM((IN_ROWS * parts,) + tile, jnp.bfloat16),
            pltpu.SemaphoreType.DMA((2, bands)),
            pltpu.SemaphoreType.DMA((IN_ROWS * parts,)),
            pltpu.SemaphoreType.DMA((3,)),
        ],
        compiler_params=pltpu.CompilerParams(
            collective_id=0, has_side_effects=True, vmem_limit_bytes=60 * 1024 * 1024
        ),
        name="exchange",
    )(frame_counts, latents.T, token_cell)
    flops = 2 * FCAP * R * W * 27 * wide * wide
    return pl.pallas_call(
        functools.partial(conv_kernel, bands, rows),
        out_shape=jax.ShapeDtypeStruct((FCAP, R, W, wide), jnp.bfloat16),
        in_specs=[hbm, vmem, hbm, hbm, hbm, hbm],
        out_specs=hbm,
        scratch_shapes=[
            pltpu.SMEM((bands,), jnp.int32),
            pltpu.VMEM((27 * channels, wide), jnp.bfloat16),
            pltpu.VMEM((wide,), jnp.float32),
            pltpu.VMEM((wide,), jnp.float32),
            pltpu.VMEM((3, IN_ROWS, IN_FRAMES, channels, W), jnp.bfloat16),
            pltpu.VMEM((MID_FRAMES, MID_ROWS, W, 3 * wide), jnp.bfloat16),
            pltpu.VMEM((3, 3 * wide, 3 * wide), jnp.bfloat16),
            pltpu.VMEM((R * W, 2 * wide), jnp.float32),
            pltpu.VMEM((FCAP, R, W, wide), jnp.bfloat16),
            pltpu.SemaphoreType.DMA((4,)),
            pltpu.SemaphoreType.DMA((3, 3)),
            pltpu.SemaphoreType.DMA((FCAP,)),
        ],
        compiler_params=pltpu.CompilerParams(vmem_limit_bytes=60 * 1024 * 1024),
        cost_estimate=pl.CostEstimate(flops=flops, bytes_accessed=12 << 20, transcendentals=0),
        name="convs",
    )(
        frame_counts,
        xin,
        in_kernel.reshape(27 * channels, wide),
        in_bias,
        mid_kernel.reshape(3, 3, 3 * wide, wide),
        mid_bias,
    )


def solution(mesh):
    placed = (P(("band", "rows"), None), P(("band", "rows")), P(), P(), P(), P(), P())
    return jax.shard_map(
        functools.partial(per_device, mesh.shape["band"], mesh.shape["rows"]),
        mesh=mesh,
        in_specs=placed,
        out_specs=P("band", "rows", None, None),
        check_vma=False,
    )
```

```python
import functools

import jax
import jax.numpy as jnp
from jax import lax
from jax.experimental import pallas as pl
from jax.experimental.pallas import tpu as pltpu
from jax.sharding import PartitionSpec as P

W = 160
R = 4
FCAP = 4
BACK = 2
IN_FRAMES = FCAP + 2 * BACK
IN_ROWS = R + 4
MID_FRAMES = FCAP + BACK
MID_ROWS = R + 2
LANES = 128
MESH = pl.DeviceIdType.MESH


def exchange_kernel(
    bands, rows, counts_in, lat_in, cell_in, out,
    counts, lat, cell, store, send, recv, send_sem, recv_sem, load_sem,
):
    loads = [
        pltpu.make_async_copy(a, b, load_sem.at[i])
        for i, (a, b) in enumerate(((cell_in, cell), (lat_in, lat), (counts_in, counts)))
    ]
    for load in loads:
        load.start()
    channels, n = lat.shape
    span = R * W // bands
    parts = W // span
    frames = n // span
    plane = R * rows * W
    band = lax.axis_index("band")
    row = lax.axis_index("rows")
    me = band * rows + row
    y = lax.div(me, parts)
    part = lax.rem(me, parts)
    home = lax.div(y, R)
    y_in = lax.rem(y, R)
    near = jnp.where(y_in < 2, home - 1, home + 1)
    near_ok = (near >= 0) & (near < rows)
    slot_home = (y_in + 2) * parts + part
    slot_near = jnp.where(y_in < 2, y_in + 6, y_in - 2) * parts + part

    def source(slot):
        src_y = R * row - 2 + slot // parts
        src = src_y * parts + slot % parts
        ok = (src_y >= 0) & (src_y < R * rows) & (src != me)
        src = jnp.maximum(src, 0)
        return lax.div(src, rows), lax.rem(src, rows), ok

    barrier = pltpu.get_barrier_semaphore()
    for slot in range(IN_ROWS * parts):
        src_band, src_row, ok = source(slot)

        @pl.when(ok)
        def _():
            pl.semaphore_signal(barrier, inc=1, device_id=(src_band, src_row), device_id_type=MESH)

    for load in loads:
        load.wait()
    cells = cell[...].reshape(1, n)
    frame = jnp.zeros_like(cells)
    for f in range(1, frames):
        frame = frame + (cells >= f * plane).astype(jnp.int32)
    lane_of = cells - frame * plane - me * span + part * span + 1
    lane_of = jnp.where(lane_of >= LANES, lane_of - LANES, lane_of)
    lat_t = lat[...].astype(jnp.float32)
    across = (((1,), (1,)), ((), ()))
    by_frame = jnp.concatenate(
        [jnp.where(frame == f, lat_t, 0.0).astype(jnp.bfloat16) for f in range(frames)], axis=0
    )
    spot = lax.broadcasted_iota(jnp.int32, (LANES, n), 0) == lane_of
    spot = jnp.where(spot, 1.0, 0.0).astype(jnp.bfloat16)
    placed = lax.dot_general(by_frame, spot, across, preferred_element_type=jnp.float32)
    store[:FCAP] = jnp.zeros((FCAP, channels, LANES), jnp.bfloat16)
    store[FCAP + frames:] = jnp.zeros((FCAP, channels, LANES), jnp.bfloat16)
    store[FCAP:FCAP + frames] = placed.astype(jnp.bfloat16).reshape(frames, channels, LANES)

    here = (home == row).astype(jnp.int32) + (near == row).astype(jnp.int32)
    total = bands + jnp.where(near_ok, bands, 0) - here
    pl.semaphore_wait(barrier, total)

    def copy_to(i, target, which, slot):
        to_band = lax.rem(band + i, bands)
        return pltpu.make_async_remote_copy(
            src_ref=send.at[i],
            dst_ref=recv.at[slot],
            send_sem=send_sem.at[which, i],
            recv_sem=recv_sem.at[slot],
            device_id=(to_band, target),
            device_id_type=MESH,
        )

    for i in range(bands):
        to_band = lax.rem(band + i, bands)
        start = jnp.int32(0)
        for q in range(bands - 1):
            start = start + jnp.where(q < to_band, counts[q], 0)
        for j in range(IN_FRAMES):
            send[i, j] = store[start + j]
        for which, target, slot, ok in ((0, home, slot_home, None), (1, near, slot_near, near_ok)):
            away = jnp.bool_(True) if i else target != row
            go = away if ok is None else away & ok

            @pl.when(go)
            def _():
                copy_to(i, target, which, slot).start()

            if i == 0:
                @pl.when(target == row)
                def _():
                    recv[slot] = send[0]

    for slot in range(IN_ROWS * parts):
        src_band, src_row, ok = source(slot)

        @pl.when(ok)
        def _():
            pltpu.make_async_remote_copy(
                src_ref=send.at[0],
                dst_ref=recv.at[slot],
                send_sem=send_sem.at[0, 0],
                recv_sem=recv_sem.at[slot],
                device_id=(src_band, src_row),
                device_id_type=MESH,
            ).wait_recv()

    lane = lax.broadcasted_iota(jnp.int32, (IN_FRAMES, channels, LANES), 2)
    for yy in range(IN_ROWS):
        at = R * row - 2 + yy
        inside = (at >= 0) & (at < R * rows)

        @pl.when(inside)
        def _():
            low = recv[yy * parts].astype(jnp.float32)
            for p in range(1, parts):
                piece = recv[yy * parts + p].astype(jnp.float32)
                low = jnp.where(lane >= p * span + 1, piece, low)
            high = jnp.where(lane < W + 1 - LANES, piece, 0.0)
            out[yy, :, :, :LANES] = low.astype(jnp.bfloat16)
            out[yy, :, :, LANES:] = high.astype(jnp.bfloat16)

        @pl.when(jnp.logical_not(inside))
        def _():
            out[yy] = jnp.zeros(out.shape[1:], jnp.bfloat16)

    for i in range(bands):
        for which, target, slot, ok in ((0, home, slot_home, None), (1, near, slot_near, near_ok)):
            away = jnp.bool_(True) if i else target != row
            go = away if ok is None else away & ok

            @pl.when(go)
            def _():
                copy_to(i, target, which, slot).wait_send()


def conv_kernel(
    bands, rows, counts_in, xin, w1_in, b1_in, w2, b2_in, out,
    counts, w1, b1, b2, xl, w1p, mid, wcat, acc, obuf, load_sem, w_sem, o_sem,
):
    loads = [
        pltpu.make_async_copy(a, b, load_sem.at[i])
        for i, (a, b) in enumerate(((counts_in, counts), (w1_in, w1), (b1_in, b1), (b2_in, b2)))
    ]
    for load in loads:
        load.start()
    channels = xin.shape[2]
    wide = w1.shape[1]
    depth = 3 * wide
    band = lax.axis_index("band")
    row = lax.axis_index("rows")

    def weight_copy(a, b):
        return pltpu.make_async_copy(
            w2.at[a, b], wcat.at[b, :, pl.ds((2 - a) * wide, wide)], w_sem.at[a, b]
        )

    for b in range(3):
        for a in range(3):
            weight_copy(a, b).start()

    half_lane = lax.broadcasted_iota(jnp.int32, (W, LANES), 1) < LANES // 2

    def spread_row(yy, carry):
        flat = xin[yy].astype(jnp.float32).reshape(IN_FRAMES * channels, 2 * LANES)
        turned = flat.T
        rolled = {k: turned if k == 0 else pltpu.roll(turned, k, 1) for k in (0, 32, 64, 96)}
        for p in range(MID_FRAMES // 2):
            even = rolled[(LANES - 32 * p) % LANES]
            odd = rolled[(LANES + 64 - 32 * p) % LANES]
            low = jnp.where(half_lane, even[:W], odd[1:W + 1])
            high = jnp.where(half_lane, even[2:W + 2], 0.0)
            xl[p, yy, :, :LANES] = low.astype(jnp.bfloat16)
            xl[p, yy, :, LANES:] = high.astype(jnp.bfloat16)
        return carry

    lax.fori_loop(0, IN_ROWS, spread_row, 0)

    for load in loads:
        load.wait()
    start = jnp.int32(0)
    for q in range(bands - 1):
        start = start + jnp.where(q < band, counts[q], 0)
    own = counts[band]

    place = lax.broadcasted_iota(jnp.int32, (8, wide), 0)
    bias1 = b1[...].reshape(1, wide)

    w1p[...] = jnp.zeros(w1p.shape, jnp.bfloat16)
    for a in range(3):
        for b in range(3):
            for e in range(3):
                tap = w1[pl.ds(((a * 3 + b) * 3 + e) * channels, channels), :]
                for k in range(2):
                    to = b * 2 * LANES + e * (LANES // 2) + (k + a) * channels
                    w1p[to:to + channels, k * wide:(k + 1) * wide] = tap

    def first(p, carry):
        for y in range(MID_ROWS):
            lhs = jnp.concatenate([xl[p, y + b] for b in range(3)], axis=1)
            both = jnp.dot(lhs, w1p[...], preferred_element_type=jnp.float32)
            for k in range(2):
                f = 2 * p + k
                finish(f, y, both[:, k * wide:(k + 1) * wide])
        return carry

    def finish(f, y, v):
        at = R * row - 1 + y
        inside = (at >= 0) & (at < R * rows) & (start - BACK + f >= 0)
        half = (v + bias1) * jnp.where(inside, 0.5, 0.0)
        active = half * jnp.tanh(half) + half
        before = pltpu.roll(active, 1, 0)
        before = jnp.concatenate([jnp.where(place == 0, 0.0, before[:8]), before[8:]], axis=0)
        after = pltpu.roll(active, W - 1, 0)
        after = jnp.concatenate([after[:-8], jnp.where(place == 7, 0.0, after[-8:])], axis=0)
        mid[f, y, :, :wide] = before.astype(jnp.bfloat16)
        mid[f, y, :, wide:2 * wide] = active.astype(jnp.bfloat16)
        mid[f, y, :, 2 * wide:] = after.astype(jnp.bfloat16)

    lax.fori_loop(0, MID_FRAMES // 2, first, 0)

    for b in range(3):
        for a in range(3):
            weight_copy(a, b).wait()

    for pair in range(FCAP // 2):
        bias = jnp.broadcast_to(b2[...].reshape(1, wide), (R * W, wide))
        acc[:, :wide] = bias
        acc[:, wide:] = bias

        def taps_of(b, carry):
            def rows_of(g):
                return mid[2 * pair + g, pl.ds(b, R)].reshape(R * W, depth)

            acc[:, :wide] += jnp.dot(
                rows_of(0), wcat[b, :, 2 * wide:], preferred_element_type=jnp.float32
            )
            acc[...] += jnp.dot(
                rows_of(1), wcat[b, :, wide:], preferred_element_type=jnp.float32
            )
            acc[...] += jnp.dot(
                rows_of(2), wcat[b, :, :2 * wide], preferred_element_type=jnp.float32
            )
            acc[:, wide:] += jnp.dot(
                rows_of(3), wcat[b, :, :wide], preferred_element_type=jnp.float32
            )
            return carry

        lax.fori_loop(0, 3, taps_of, 0)
        for k in range(2):
            t = 2 * pair + k
            value = acc[:, k * wide:(k + 1) * wide]
            value = jnp.where(t < own, value, 0.0).astype(jnp.bfloat16)
            obuf[t] = value.reshape(R, W, wide)
            pltpu.make_async_copy(obuf.at[t], out.at[t], o_sem.at[t]).start()
    for t in range(FCAP):
        pltpu.make_async_copy(obuf.at[t], out.at[t], o_sem.at[t]).wait()


def per_device(bands, rows, latents, token_cell, frame_counts, in_kernel, in_bias, mid_kernel, mid_bias):
    n, channels = latents.shape
    wide = in_kernel.shape[-1]
    span = R * W // bands
    parts = W // span
    frames = n // span
    vmem = pl.BlockSpec(memory_space=pltpu.VMEM)
    hbm = pl.BlockSpec(memory_space=pltpu.HBM)
    tile = (IN_FRAMES, channels, LANES)
    xin = pl.pallas_call(
        functools.partial(exchange_kernel, bands, rows),
        out_shape=jax.ShapeDtypeStruct((IN_ROWS, IN_FRAMES, channels, 2 * LANES), jnp.bfloat16),
        in_specs=[hbm] * 3,
        out_specs=vmem,
        scratch_shapes=[
            pltpu.SMEM((bands,), jnp.int32),
            pltpu.VMEM((channels, n), jnp.bfloat16),
            pltpu.VMEM((n,), jnp.int32),
            pltpu.VMEM((frames + 2 * FCAP, channels, LANES), jnp.bfloat16),
            pltpu.VMEM((bands,) + tile, jnp.bfloat16),
            pltpu.VMEM((IN_ROWS * parts,) + tile, jnp.bfloat16),
            pltpu.SemaphoreType.DMA((2, bands)),
            pltpu.SemaphoreType.DMA((IN_ROWS * parts,)),
            pltpu.SemaphoreType.DMA((3,)),
        ],
        compiler_params=pltpu.CompilerParams(
            collective_id=0, has_side_effects=True, vmem_limit_bytes=60 * 1024 * 1024
        ),
        name="exchange",
    )(frame_counts, latents.T, token_cell)
    flops = 2 * FCAP * R * W * 27 * wide * wide
    return pl.pallas_call(
        functools.partial(conv_kernel, bands, rows),
        out_shape=jax.ShapeDtypeStruct((FCAP, R, W, wide), jnp.bfloat16),
        in_specs=[hbm, vmem, hbm, hbm, hbm, hbm],
        out_specs=hbm,
        scratch_shapes=[
            pltpu.SMEM((bands,), jnp.int32),
            pltpu.VMEM((27 * channels, wide), jnp.bfloat16),
            pltpu.VMEM((wide,), jnp.float32),
            pltpu.VMEM((wide,), jnp.float32),
            pltpu.VMEM((MID_FRAMES // 2, IN_ROWS, W, 2 * LANES), jnp.bfloat16),
            pltpu.VMEM((6 * LANES, 2 * wide), jnp.bfloat16),
            pltpu.VMEM((MID_FRAMES, MID_ROWS, W, 3 * wide), jnp.bfloat16),
            pltpu.VMEM((3, 3 * wide, 3 * wide), jnp.bfloat16),
            pltpu.VMEM((R * W, 2 * wide), jnp.float32),
            pltpu.VMEM((FCAP, R, W, wide), jnp.bfloat16),
            pltpu.SemaphoreType.DMA((4,)),
            pltpu.SemaphoreType.DMA((3, 3)),
            pltpu.SemaphoreType.DMA((FCAP,)),
        ],
        compiler_params=pltpu.CompilerParams(vmem_limit_bytes=60 * 1024 * 1024),
        cost_estimate=pl.CostEstimate(flops=flops, bytes_accessed=12 << 20, transcendentals=0),
        name="convs",
    )(
        frame_counts,
        xin,
        in_kernel.reshape(27 * channels, wide),
        in_bias,
        mid_kernel.reshape(3, 3, 3 * wide, wide),
        mid_bias,
    )


def solution(mesh):
    placed = (P(("band", "rows"), None), P(("band", "rows")), P(), P(), P(), P(), P())
    return jax.shard_map(
        functools.partial(per_device, mesh.shape["band"], mesh.shape["rows"]),
        mesh=mesh,
        in_specs=placed,
        out_specs=P("band", "rows", None, None),
        check_vma=False,
    )
```

```python
import functools

import jax
import jax.numpy as jnp
from jax import lax
from jax.experimental import pallas as pl
from jax.experimental.pallas import tpu as pltpu
from jax.sharding import PartitionSpec as P

W = 160
R = 4
FCAP = 4
BACK = 2
IN_FRAMES = FCAP + 2 * BACK
IN_ROWS = R + 4
MID_FRAMES = FCAP + BACK
MID_ROWS = R + 2
LANES = 128
MESH = pl.DeviceIdType.MESH


def exchange_kernel(
    bands, rows, counts_in, lat_in, cell_in, out,
    counts, lat, cell, store, send, recv, send_sem, recv_sem, load_sem,
):
    loads = [
        pltpu.make_async_copy(a, b, load_sem.at[i])
        for i, (a, b) in enumerate(((cell_in, cell), (lat_in, lat), (counts_in, counts)))
    ]
    for load in loads:
        load.start()
    channels, n = lat.shape
    span = R * W // bands
    parts = W // span
    frames = n // span
    plane = R * rows * W
    band = lax.axis_index("band")
    row = lax.axis_index("rows")
    me = band * rows + row
    y = lax.div(me, parts)
    part = lax.rem(me, parts)
    home = lax.div(y, R)
    y_in = lax.rem(y, R)
    near = jnp.where(y_in < 2, home - 1, home + 1)
    near_ok = (near >= 0) & (near < rows)
    slot_home = (y_in + 2) * parts + part
    slot_near = jnp.where(y_in < 2, y_in + 6, y_in - 2) * parts + part

    def source(slot):
        src_y = R * row - 2 + slot // parts
        src = src_y * parts + slot % parts
        ok = (src_y >= 0) & (src_y < R * rows) & (src != me)
        src = jnp.maximum(src, 0)
        return lax.div(src, rows), lax.rem(src, rows), ok

    barrier = pltpu.get_barrier_semaphore()
    for slot in range(IN_ROWS * parts):
        src_band, src_row, ok = source(slot)

        @pl.when(ok)
        def _():
            pl.semaphore_signal(barrier, inc=1, device_id=(src_band, src_row), device_id_type=MESH)

    for load in loads:
        load.wait()
    cells = cell[...].reshape(1, n)
    frame = jnp.zeros_like(cells)
    for f in range(1, frames):
        frame = frame + (cells >= f * plane).astype(jnp.int32)
    lane_of = cells - frame * plane - me * span
    lat_t = lat[...].astype(jnp.float32)
    across = (((1,), (1,)), ((), ()))
    by_frame = jnp.concatenate(
        [jnp.where(frame == f, lat_t, 0.0).astype(jnp.bfloat16) for f in range(frames)], axis=0
    )
    spot = lax.broadcasted_iota(jnp.int32, (LANES, n), 0) == lane_of
    spot = jnp.where(spot, 1.0, 0.0).astype(jnp.bfloat16)
    placed = lax.dot_general(by_frame, spot, across, preferred_element_type=jnp.float32)
    store[:FCAP] = jnp.zeros((FCAP, channels, LANES), jnp.bfloat16)
    store[FCAP + frames:] = jnp.zeros((FCAP, channels, LANES), jnp.bfloat16)
    store[FCAP:FCAP + frames] = placed.astype(jnp.bfloat16).reshape(frames, channels, LANES)

    here = (home == row).astype(jnp.int32) + (near == row).astype(jnp.int32)
    total = bands + jnp.where(near_ok, bands, 0) - here
    pl.semaphore_wait(barrier, total)

    packed = send.shape[2]
    lane = lax.broadcasted_iota(jnp.int32, (channels, LANES), 1)

    def copy_to(i, target, which, slot):
        to_band = lax.rem(band + i, bands)
        return pltpu.make_async_remote_copy(
            src_ref=send.at[i],
            dst_ref=recv.at[slot],
            send_sem=send_sem.at[which, i],
            recv_sem=recv_sem.at[slot],
            device_id=(to_band, target),
            device_id_type=MESH,
        )

    for i in range(bands):
        to_band = lax.rem(band + i, bands)
        start = jnp.int32(0)
        for q in range(bands - 1):
            start = start + jnp.where(q < to_band, counts[q], 0)
        tiles = [jnp.zeros((channels, LANES), jnp.float32)] * (packed // LANES)
        for j in range(IN_FRAMES):
            m, by = divmod(span * j, LANES)
            piece = store[start + j].astype(jnp.float32)
            piece = pltpu.roll(piece, by, 1) if by else piece
            if by + span > LANES:
                tiles[m + 1] = jnp.where(lane < by, piece, tiles[m + 1])
            tiles[m] = jnp.where(lane >= by, piece, tiles[m]) if by else piece
        send[i] = jnp.concatenate(tiles, axis=1).astype(jnp.bfloat16)
        for which, target, slot, ok in ((0, home, slot_home, None), (1, near, slot_near, near_ok)):
            away = jnp.bool_(True) if i else target != row
            go = away if ok is None else away & ok

            @pl.when(go)
            def _():
                copy_to(i, target, which, slot).start()

            if i == 0:
                @pl.when(target == row)
                def _():
                    recv[slot] = send[0]

    for slot in range(IN_ROWS * parts):
        src_band, src_row, ok = source(slot)

        @pl.when(ok)
        def _():
            pltpu.make_async_remote_copy(
                src_ref=send.at[0],
                dst_ref=recv.at[slot],
                send_sem=send_sem.at[0, 0],
                recv_sem=recv_sem.at[slot],
                device_id=(src_band, src_row),
                device_id_type=MESH,
            ).wait_recv()

    for yy in range(IN_ROWS):
        at = R * row - 2 + yy
        inside = (at >= 0) & (at < R * rows)

        @pl.when(inside)
        def _():
            rows_in = [recv[yy * parts + p].astype(jnp.float32) for p in range(parts)]
            for j in range(IN_FRAMES):
                m, by = divmod(span * j, LANES)
                low = jnp.zeros((channels, LANES), jnp.float32)
                for p in range(parts):
                    piece = rows_in[p][:, m * LANES:(m + 1) * LANES]
                    if by + span > LANES:
                        over = rows_in[p][:, (m + 1) * LANES:(m + 2) * LANES]
                        piece = jnp.where(lane >= by, piece, over)
                    to = p * span + 1
                    turn = (to - by) % LANES
                    piece = pltpu.roll(piece, turn, 1) if turn else piece
                    low = jnp.where(lane >= to, piece, low)
                high = jnp.where(lane < W + 1 - LANES, piece, 0.0)
                out[yy, j, :, :LANES] = low.astype(jnp.bfloat16)
                out[yy, j, :, LANES:] = high.astype(jnp.bfloat16)

        @pl.when(jnp.logical_not(inside))
        def _():
            out[yy] = jnp.zeros(out.shape[1:], jnp.bfloat16)

    for i in range(bands):
        for which, target, slot, ok in ((0, home, slot_home, None), (1, near, slot_near, near_ok)):
            away = jnp.bool_(True) if i else target != row
            go = away if ok is None else away & ok

            @pl.when(go)
            def _():
                copy_to(i, target, which, slot).wait_send()


def conv_kernel(
    bands, rows, counts_in, xin, w1_in, b1_in, w2, b2_in, out,
    counts, w1, b1, b2, xl, w1p, mid, wcat, acc, obuf, load_sem, w_sem, o_sem,
):
    loads = [
        pltpu.make_async_copy(a, b, load_sem.at[i])
        for i, (a, b) in enumerate(((counts_in, counts), (w1_in, w1), (b1_in, b1), (b2_in, b2)))
    ]
    for load in loads:
        load.start()
    channels = xin.shape[2]
    wide = w1.shape[1]
    depth = 3 * wide
    band = lax.axis_index("band")
    row = lax.axis_index("rows")

    def weight_copy(a, b):
        return pltpu.make_async_copy(
            w2.at[a, b], wcat.at[pl.ds(b * depth, depth), pl.ds((2 - a) * wide, wide)], w_sem.at[a, b]
        )

    for b in range(3):
        for a in range(3):
            weight_copy(a, b).start()

    half_lane = lax.broadcasted_iota(jnp.int32, (W, LANES), 1) < LANES // 2

    def spread_row(yy, carry):
        flat = xin[yy].astype(jnp.float32).reshape(IN_FRAMES * channels, 2 * LANES)
        turned = flat.T
        rolled = {k: turned if k == 0 else pltpu.roll(turned, k, 1) for k in (0, 32, 64, 96)}
        for p in range(MID_FRAMES // 2):
            even = rolled[(LANES - 32 * p) % LANES]
            odd = rolled[(LANES + 64 - 32 * p) % LANES]
            low = jnp.where(half_lane, even[:W], odd[1:W + 1])
            high = jnp.where(half_lane, even[2:W + 2], 0.0)
            xl[p, yy, :, :LANES] = low.astype(jnp.bfloat16)
            xl[p, yy, :, LANES:] = high.astype(jnp.bfloat16)
        return carry

    lax.fori_loop(0, IN_ROWS, spread_row, 0)

    for load in loads:
        load.wait()
    start = jnp.int32(0)
    for q in range(bands - 1):
        start = start + jnp.where(q < band, counts[q], 0)
    own = counts[band]

    place = lax.broadcasted_iota(jnp.int32, (8, wide), 0)
    bias1 = b1[...].reshape(1, wide)

    w1p[...] = jnp.zeros(w1p.shape, jnp.bfloat16)
    for a in range(3):
        for b in range(3):
            for e in range(3):
                tap = w1[pl.ds(((a * 3 + b) * 3 + e) * channels, channels), :]
                for k in range(2):
                    to = b * 2 * LANES + e * (LANES // 2) + (k + a) * channels
                    w1p[to:to + channels, k * wide:(k + 1) * wide] = tap

    def first(p, carry):
        for y in range(MID_ROWS):
            lhs = jnp.concatenate([xl[p, y + b] for b in range(3)], axis=1)
            both = jnp.dot(lhs, w1p[...], preferred_element_type=jnp.float32)
            for k in range(2):
                f = 2 * p + k
                finish(f, y, both[:, k * wide:(k + 1) * wide])
        return carry

    def finish(f, y, v):
        at = R * row - 1 + y
        inside = (at >= 0) & (at < R * rows) & (start - BACK + f >= 0)
        half = (v + bias1) * jnp.where(inside, 0.5, 0.0)
        active = half * jnp.tanh(half) + half
        before = pltpu.roll(active, 1, 0)
        before = jnp.concatenate([jnp.where(place == 0, 0.0, before[:8]), before[8:]], axis=0)
        after = pltpu.roll(active, W - 1, 0)
        after = jnp.concatenate([after[:-8], jnp.where(place == 7, 0.0, after[-8:])], axis=0)
        for e, tap in enumerate((before, active, after)):
            tap = tap.astype(jnp.bfloat16)
            for b in range(max(0, y - R + 1), min(3, y + 1)):
                at_lane = b * depth + e * wide
                mid[f, y - b, :, at_lane:at_lane + wide] = tap

    lax.fori_loop(0, MID_FRAMES // 2, first, 0)

    for b in range(3):
        for a in range(3):
            weight_copy(a, b).wait()

    bias2 = b2[...].reshape(1, wide)

    def mix(pair, carry):
        def product(g, first_tap, last_tap):
            lhs = mid[2 * pair + g].reshape(R * W, 3 * depth)
            rhs = wcat[:, first_tap * wide:last_tap * wide]
            return jnp.dot(lhs, rhs, preferred_element_type=jnp.float32)

        acc[...] = product(1, 1, 3)
        acc[...] += product(2, 0, 2)
        for k, g, tap in ((0, 0, 2), (1, 3, 0)):
            t = 2 * pair + k
            value = acc[:, k * wide:(k + 1) * wide] + product(g, tap, tap + 1) + bias2
            value = jnp.where(t < own, value, 0.0).astype(jnp.bfloat16)
            obuf[t] = value.reshape(R, W, wide)
            pltpu.make_async_copy(obuf.at[t], out.at[t], o_sem.at[t]).start()
        return carry

    lax.fori_loop(0, FCAP // 2, mix, 0)
    for t in range(FCAP):
        pltpu.make_async_copy(obuf.at[t], out.at[t], o_sem.at[t]).wait()


def per_device(bands, rows, latents, token_cell, frame_counts, in_kernel, in_bias, mid_kernel, mid_bias):
    n, channels = latents.shape
    wide = in_kernel.shape[-1]
    span = R * W // bands
    parts = W // span
    frames = n // span
    vmem = pl.BlockSpec(memory_space=pltpu.VMEM)
    hbm = pl.BlockSpec(memory_space=pltpu.HBM)
    tile = (channels, -(-IN_FRAMES * span // LANES) * LANES)
    xin = pl.pallas_call(
        functools.partial(exchange_kernel, bands, rows),
        out_shape=jax.ShapeDtypeStruct((IN_ROWS, IN_FRAMES, channels, 2 * LANES), jnp.bfloat16),
        in_specs=[hbm] * 3,
        out_specs=vmem,
        scratch_shapes=[
            pltpu.SMEM((bands,), jnp.int32),
            pltpu.VMEM((channels, n), jnp.bfloat16),
            pltpu.VMEM((n,), jnp.int32),
            pltpu.VMEM((frames + 2 * FCAP, channels, LANES), jnp.bfloat16),
            pltpu.VMEM((bands,) + tile, jnp.bfloat16),
            pltpu.VMEM((IN_ROWS * parts,) + tile, jnp.bfloat16),
            pltpu.SemaphoreType.DMA((2, bands)),
            pltpu.SemaphoreType.DMA((IN_ROWS * parts,)),
            pltpu.SemaphoreType.DMA((3,)),
        ],
        compiler_params=pltpu.CompilerParams(
            collective_id=0, has_side_effects=True, vmem_limit_bytes=60 * 1024 * 1024
        ),
        name="exchange",
    )(frame_counts, latents.T, token_cell)
    flops = 2 * FCAP * R * W * 27 * wide * wide
    return pl.pallas_call(
        functools.partial(conv_kernel, bands, rows),
        out_shape=jax.ShapeDtypeStruct((FCAP, R, W, wide), jnp.bfloat16),
        in_specs=[hbm, vmem, hbm, hbm, hbm, hbm],
        out_specs=hbm,
        scratch_shapes=[
            pltpu.SMEM((bands,), jnp.int32),
            pltpu.VMEM((27 * channels, wide), jnp.bfloat16),
            pltpu.VMEM((wide,), jnp.float32),
            pltpu.VMEM((wide,), jnp.float32),
            pltpu.VMEM((MID_FRAMES // 2, IN_ROWS, W, 2 * LANES), jnp.bfloat16),
            pltpu.VMEM((6 * LANES, 2 * wide), jnp.bfloat16),
            pltpu.VMEM((MID_FRAMES, R, W, 9 * wide), jnp.bfloat16),
            pltpu.VMEM((9 * wide, 3 * wide), jnp.bfloat16),
            pltpu.VMEM((R * W, 2 * wide), jnp.float32),
            pltpu.VMEM((FCAP, R, W, wide), jnp.bfloat16),
            pltpu.SemaphoreType.DMA((4,)),
            pltpu.SemaphoreType.DMA((3, 3)),
            pltpu.SemaphoreType.DMA((FCAP,)),
        ],
        compiler_params=pltpu.CompilerParams(vmem_limit_bytes=60 * 1024 * 1024),
        cost_estimate=pl.CostEstimate(flops=flops, bytes_accessed=12 << 20, transcendentals=0),
        name="convs",
    )(
        frame_counts,
        xin,
        in_kernel.reshape(27 * channels, wide),
        in_bias,
        mid_kernel.reshape(3, 3, 3 * wide, wide),
        mid_bias,
    )


def solution(mesh):
    placed = (P(("band", "rows"), None), P(("band", "rows")), P(), P(), P(), P(), P())
    return jax.shard_map(
        functools.partial(per_device, mesh.shape["band"], mesh.shape["rows"]),
        mesh=mesh,
        in_specs=placed,
        out_specs=P("band", "rows", None, None),
        check_vma=False,
    )
```
